32 devices in a mesh: row: 4 (over y, core), col: 8 (over z, x).
Axes of the slice: x: 2, y: 2, z: 4, core: 2. Of those that a mesh axis runs over, the one named last changes fastest.
Arguments:
- left: bfloat16 [8, 16, 512, 256], P('row', 'col'), may hold values from -0.11767578 to 0.11767578
- right: bfloat16 [8, 16, 512, 256], P('row', 'col'), may hold values from -6 to 6
- lower_inverse: bfloat16 [2, 512, 512], P(None, 'row'), as said below
- upper_inverse: bfloat16 [2, 512, 512], P(None, None, 'col'), as said below
- ranks: int32 [8, 16], P('row', 'col'), may hold values from 16 to 256, as said below
Outputs:
- right_out: bfloat16 [8, 16, 512, 256], P('row', 'col')
The draws below stay inside these ranges and needn't reach their ends.
Inputs may be any that keep to these rules, and one draw needn't show every extreme that they name: Tile ranks: every row of `ranks` contains at least one entry equal to 256; all entries lie in 4..256. Each lower_inverse[k] is lower triangular with a positive diagonal. Each upper_inverse[k] is upper triangular with a positive diagonal.
All inputs are finite; a program needn't handle non-finite values.
Results may differ from the reference program's by a relative error of at most 0.009.
Values may be sent and summed in bfloat16 or wider, within the bound.
A program may use at most 64 MiB of HBM per device.

```python
import jax
import jax.numpy as jnp
from jax import lax

B = 512
R = 256
TR_DEV = 2
TC_DEV = 2
PANELS = 2
NTR = 8
NTC = 16
N_ROW = 4
N_COL = 8


def triangle_draw(key, lower):
    noise_key, diag_key = jax.random.split(jax.random.fold_in(key, 7))
    noise = jax.random.normal(noise_key, (PANELS, B, B), jnp.float32)
    noise = noise * (0.5 * B ** (-0.5))
    diag = jax.random.uniform(diag_key, (PANELS, B, 1), jnp.float32, 0.8, 1.25)
    index = jnp.arange(B, dtype=jnp.int32)
    eye = index[:, None] == index[None, :]
    if lower:
        below = index[:, None] > index[None, :]
    else:
        below = index[:, None] < index[None, :]
    full = jnp.where(eye[None], diag, jnp.where(below[None], noise, 0.0))
    return full.astype(jnp.bfloat16)


def draw_lower_inverse(key, part):
    return triangle_draw(jax.random.fold_in(key, 11), True)


def draw_upper_inverse(key, part):
    return triangle_draw(jax.random.fold_in(key, 13), False)


def draw_ranks(key, part):
    first, second = jax.random.split(jax.random.fold_in(key, 17))
    values = jax.random.randint(first, (NTR, NTC), R // 16, R + 1, jnp.int32)
    chosen = jax.random.randint(second, (NTR,), 0, NTC, jnp.int32)
    columns = jnp.arange(NTC, dtype=jnp.int32)
    return jnp.where(columns[None, :] == chosen[:, None], R, values).astype(jnp.int32)


def block_scale(key, extent, shards, least, high):
    level, own = 1.0, jax.random.fold_in(key, 6)
    for axis_at, parts in shards:
        heights = jnp.exp(jax.random.uniform(jax.random.fold_in(own, axis_at), (parts,), jnp.float32, least / len(shards), high / len(shards)))
        level = level * jnp.repeat(heights, extent[axis_at] // parts).reshape([-1 if axis == axis_at else 1 for axis in range(len(extent))])
    return level


def gaussian(own_key, shape, scale, most, shards=(), held_as=jnp.bfloat16):
    loudness = block_scale(own_key, shape, shards, -0.22, 0.18) if shards else 1.0
    array = jax.random.normal(own_key, shape, jnp.float32) * scale * loudness
    return jnp.minimum(jnp.maximum(array, -most), most).astype(held_as)


def setup_inputs(seed: int = 0) -> dict:
    key_list = jax.random.split(jax.random.key(seed), 6)
    left = gaussian(key_list[0], (NTR, NTC, B, R), ((R * B) ** -0.3333), 0.11767578, ((0, 4), (1, 8)))
    right = gaussian(key_list[1], (NTR, NTC, B, R), 1.0, 6.0, ((0, 4), (1, 8)))
    lower_inverse = draw_lower_inverse(jax.random.fold_in(key_list[5], 71), 0)
    upper_inverse = draw_upper_inverse(jax.random.fold_in(key_list[5], 71), 0)
    ranks = draw_ranks(jax.random.fold_in(key_list[5], 71), 0)
    return {"left": left, "right": right, "lower_inverse": lower_inverse, "upper_inverse": upper_inverse, "ranks": ranks}


def to_tiles(stored):
    rest = stored.shape[2:]
    grid = stored.reshape((N_ROW, TR_DEV, N_COL, TC_DEV) + rest)
    order = (1, 0, 3, 2) + tuple(range(4, 4 + len(rest)))
    return jnp.transpose(grid, order).reshape((NTR, NTC) + rest)


def from_tiles(tiles):
    rest = tiles.shape[2:]
    grid = tiles.reshape((TR_DEV, N_ROW, TC_DEV, N_COL) + rest)
    order = (1, 0, 3, 2) + tuple(range(4, 4 + len(rest)))
    return jnp.transpose(grid, order).reshape((NTR, NTC) + rest)


def reference(left, right, lower_inverse, upper_inverse, ranks):
    slots = jnp.arange(R, dtype=jnp.int32)
    keep = (slots[None, None, :] < ranks[:, :, None]).astype(jnp.bfloat16)
    left = to_tiles(left * keep[:, :, None, :])
    right = to_tiles(right * keep[:, :, None, :])
    columns = jnp.arange(NTC, dtype=jnp.int32)
    for panel in range(PANELS):
        col_left = left[:, panel]
        col_right = jnp.einsum('bc,ibr->icr', upper_inverse[panel].astype(jnp.float32), right[:, panel].astype(jnp.float32)).astype(jnp.bfloat16)
        row_left = jnp.einsum('cb,jbr->jcr', lower_inverse[panel].astype(jnp.float32), left[panel].astype(jnp.float32)).astype(jnp.bfloat16)
        row_right = right[panel].astype(jnp.float32)

        def one_row(items):
            tile_left, tile_right, own_left, own_right, index = items
            core = jnp.einsum('br,jbs->jrs', own_right.astype(jnp.float32), row_left.astype(jnp.float32))
            intersection = jnp.einsum('jbr,bs->jrs', tile_left.astype(jnp.float32), own_left.astype(jnp.float32))
            mixed = jnp.einsum('jrs,jst->jrt', intersection, core, precision=lax.Precision.HIGHEST).astype(jnp.bfloat16)
            change = jnp.einsum('jbt,jrt->jbr', row_right, mixed.astype(jnp.float32))
            fresh = (tile_right.astype(jnp.float32) - change).astype(jnp.bfloat16)
            trail = (index > panel) & (columns > panel)
            on_panel = (index > panel) & (columns == panel)
            kept = jnp.where(on_panel[:, None, None], own_right[None], tile_right)
            return jnp.where(trail[:, None, None], fresh, kept)

        right = lax.map(one_row, (left, right, col_left, col_right, jnp.arange(NTR, dtype=jnp.int32)))
    return from_tiles(right)
```

```python
import functools

import jax
import jax.numpy as jnp
from jax import lax
from jax.experimental import pallas as pl
from jax.experimental.pallas import tpu as pltpu
from jax.sharding import PartitionSpec as P

CHUNKS = 4
MESH = pl.DeviceIdType.MESH


def matmul(a, b):
    return jnp.dot(a, b, preferred_element_type=jnp.float32)


def matmul_tn(a, b):
    return lax.dot_general(a, b, (((0,), (0,)), ((), ())), preferred_element_type=jnp.float32)


def matmul_nt(a, b):
    return lax.dot_general(a, b, (((1,), (1,)), ((), ())), preferred_element_type=jnp.float32)


def children(index, extent, minor, source):
    x, m = lax.rem(index, minor), lax.div(index, minor)
    found = [((x == source) & (m + 1 < extent // minor), index + minor)]
    if source + 1 < minor:
        found.append(((x >= source) & (x + 1 < minor), index + 1))
    if source > 0:
        found.append(((x <= source) & (x >= 1), index - 1))
    return found


def kernel(
    n_row, n_col, minor_col, ranks, left, right, lower, upper, out,
    ul, col_u, col_y, row_y, row_u, low, up,
    send_sem, recv_sem, inv_send, low_recv, up_recv,
):
    r, c = lax.axis_index("row"), lax.axis_index("col")
    order, width = left.shape[2], left.shape[3]
    step = order // CHUNKS
    barrier = pltpu.get_barrier_semaphore()
    for d in range(1, n_row):
        pl.semaphore_signal(
            barrier, inc=1, device_id={"row": lax.rem(r + d, n_row)}, device_id_type=MESH
        )
    for d in range(1, n_col):
        pl.semaphore_signal(
            barrier, inc=1, device_id={"col": lax.rem(c + d, n_col)}, device_id_type=MESH
        )

    lanes = lax.broadcasted_iota(jnp.int32, (1, width), 1)

    def keep(a, b):
        return (lanes < ranks[a, b]).astype(jnp.float32).astype(jnp.bfloat16)

    for a in range(2):
        for b in range(2):
            mask = keep(a, b)
            ul[a, b] = left[a, b] * mask
            out[a, b] = right[a, b] * mask
    for k in range(2):

        @pl.when(c == k)
        def _():
            up[pl.ds(k * upper.shape[1], upper.shape[1])] = upper[k]
            for a in range(2):
                col_u[k, a] = ul[a, 0]

        @pl.when(r == k)
        def _():
            low[pl.ds(k * lower.shape[1], lower.shape[1])] = lower[k]
            if k == 0:
                for b in range(2):
                    row_y[0, b] = out[0, b]

    pl.semaphore_wait(barrier, n_row - 1 + n_col - 1)

    buffers = {"cu": col_u, "cy": col_y, "ru": row_u, "ry": row_y}
    place = {
        (kind, k, t): n
        for n, (kind, k, t) in enumerate(
            (kind, k, t) for kind in ("cu", "cy", "ru", "ry") for k in range(2) for t in range(2)
        )
    }
    started = []

    def axis_of(item):
        return "col" if item[0][0] == "c" else "row"

    def tree(item):
        if axis_of(item) == "col":
            return children(c, n_col, minor_col, item[1])
        return children(r, n_row, 2, item[1])

    def copy_of(item, chunk, way, target):
        kind, k, t = item
        view = buffers[kind].at[k, t, pl.ds(chunk * step, step)]
        return pltpu.make_async_remote_copy(
            src_ref=view,
            dst_ref=view,
            send_sem=send_sem.at[place[item], chunk, way],
            recv_sem=recv_sem.at[place[item], chunk],
            device_id={axis_of(item): target},
            device_id_type=MESH,
        )

    def push(item, chunk):
        for way, (needed, target) in enumerate(tree(item)):

            @pl.when(needed)
            def _():
                copy_of(item, chunk, way, target).start()

        started.append((item, chunk))

    def is_source(item):
        return (c if axis_of(item) == "col" else r) == item[1]

    def send(item):
        @pl.when(is_source(item))
        def _():
            for chunk in range(CHUNKS):
                for way, (needed, target) in enumerate(tree(item)):

                    @pl.when(needed)
                    def _():
                        copy_of(item, chunk, way, target).start()

    def relay(items):
        for chunk in range(CHUNKS):
            for item in items:

                @pl.when(jnp.logical_not(is_source(item)))
                def _():
                    copy_of(item, chunk, 0, 0).wait_recv()
                    for way, (needed, target) in enumerate(tree(item)):

                        @pl.when(needed)
                        def _():
                            copy_of(item, chunk, way, target).start()

    def up_copy(k, source):
        rows = upper.shape[1]
        return pltpu.make_async_remote_copy(
            src_ref=upper.at[k],
            dst_ref=up.at[pl.ds(pl.multiple_of(source * rows, rows), rows)],
            send_sem=inv_send.at[0, k],
            recv_sem=up_recv.at[source],
            device_id={"col": k},
            device_id_type=MESH,
        )

    def low_copy(k, source):
        rows = lower.shape[1]
        return pltpu.make_async_remote_copy(
            src_ref=lower.at[k],
            dst_ref=low.at[pl.ds(pl.multiple_of(source * rows, rows), rows)],
            send_sem=inv_send.at[1, k],
            recv_sem=low_recv.at[source],
            device_id={"row": k},
            device_id_type=MESH,
        )

    for k in range(2):

        @pl.when(c != k)
        def _():
            up_copy(k, c).start()

        @pl.when(r != k)
        def _():
            low_copy(k, r).start()

    send(("cu", 0, 0))
    send(("cu", 1, 0))
    for b in range(2):
        send(("ry", 0, b))

    @pl.when(c < 2)
    def _():
        for s in range(n_col):

            @pl.when(s != c)
            def _():
                up_copy(0, s).wait_recv()

    @pl.when(c == 0)
    def _():
        col_y[0, 0] = matmul(up[...], out[0, 0]).astype(jnp.bfloat16)

    send(("cy", 0, 0))
    send(("cu", 0, 1))
    send(("cu", 1, 1))

    @pl.when(c == 0)
    def _():
        col_y[0, 1] = matmul(up[...], out[1, 0]).astype(jnp.bfloat16)

    send(("cy", 0, 1))

    @pl.when(r < 2)
    def _():
        for s in range(n_row):

            @pl.when(s != r)
            def _():
                low_copy(0, s).wait_recv()

    for b in range(2):
        for k in range(2):

            @pl.when(r == k)
            def _():
                row_u[k, b] = matmul(low[...], ul[0, b]).astype(jnp.bfloat16)

            send(("ru", k, b))

    def update(panel, a):
        row_in = (a * n_row + r) > panel
        for b in range(2):
            tile_col = b * n_col + c

            @pl.when(row_in & (tile_col > panel))
            def _():
                core = matmul_tn(col_y[panel, a], row_u[panel, b]).astype(jnp.bfloat16)
                meet = matmul_tn(ul[a, b], col_u[panel, a]).astype(jnp.bfloat16)
                mixed = matmul(meet, core).astype(jnp.bfloat16)
                change = matmul_nt(row_y[panel, b], mixed)
                out[a, b] = (out[a, b].astype(jnp.float32) - change).astype(jnp.bfloat16)

        @pl.when(row_in & (c == panel))
        def _():
            out[a, 0] = col_y[panel, a]

    def solve_next(a):
        @pl.when(c == 1)
        def _():
            col_y[1, a] = matmul(up[...], out[a, 0]).astype(jnp.bfloat16)

        send(("cy", 1, a))

    relay([("cu", 0, 0), ("cu", 1, 0), ("ry", 0, 0), ("ry", 0, 1)])
    relay([("cy", 0, 0), ("ru", 0, 0), ("ru", 0, 1)])
    update(0, 0)
    solve_next(0)

    @pl.when(r == 1)
    def _():
        for b in range(2):
            row_y[1, b] = out[0, b]

    for b in range(2):
        send(("ry", 1, b))
    relay([("cu", 0, 1), ("cu", 1, 1), ("ru", 1, 0)])
    relay([("cy", 0, 1), ("ru", 1, 1)])
    update(0, 1)
    solve_next(1)
    relay([("cy", 1, 0), ("ry", 1, 0), ("ry", 1, 1)])
    update(1, 0)
    relay([("cy", 1, 1)])
    update(1, 1)

    for k in range(2):

        @pl.when(c != k)
        def _():
            up_copy(k, c).wait_send()

        @pl.when(r != k)
        def _():
            low_copy(k, r).wait_send()

    for item in place:
        for way, (needed, target) in enumerate(tree(item)):

            @pl.when(needed)
            def _():
                for chunk in range(CHUNKS):
                    copy_of(item, chunk, way, target).wait_send()


def body(left, right, lower_inverse, upper_inverse, ranks):
    n_row, n_col = lax.axis_size("row"), lax.axis_size("col")
    minor_col = 4 if n_col % 4 == 0 and n_col > 8 else 2
    order, width = left.shape[2:]
    upper = jnp.swapaxes(upper_inverse, 1, 2)
    tile = (order, width)
    vmem = pl.BlockSpec(memory_space=pltpu.VMEM)
    return pl.pallas_call(
        functools.partial(kernel, n_row, n_col, minor_col),
        out_shape=jax.ShapeDtypeStruct(right.shape, jnp.bfloat16),
        in_specs=[pl.BlockSpec(memory_space=pltpu.SMEM)] + [vmem] * 4,
        out_specs=vmem,
        scratch_shapes=[
            pltpu.VMEM((2, 2) + tile, jnp.bfloat16),
            pltpu.VMEM((2, 2) + tile, jnp.bfloat16),
            pltpu.VMEM((2, 2) + tile, jnp.bfloat16),
            pltpu.VMEM((2, 2) + tile, jnp.bfloat16),
            pltpu.VMEM((2, 2) + tile, jnp.bfloat16),
            pltpu.VMEM((order, order), jnp.bfloat16),
            pltpu.VMEM((order, order), jnp.bfloat16),
            pltpu.SemaphoreType.DMA((16, CHUNKS, 3)),
            pltpu.SemaphoreType.DMA((16, CHUNKS)),
            pltpu.SemaphoreType.DMA((2, 2)),
            pltpu.SemaphoreType.DMA((n_row,)),
            pltpu.SemaphoreType.DMA((n_col,)),
        ],
        compiler_params=pltpu.CompilerParams(
            collective_id=0, has_side_effects=True, vmem_limit_bytes=40 * 1024 * 1024
        ),
        cost_estimate=pl.CostEstimate(
            flops=2_000_000_000, bytes_accessed=4_000_000, transcendentals=0
        ),
    )(ranks, left, right, lower_inverse, upper)


def solution(mesh):
    placed = (
        P("row", "col", None, None),
        P("row", "col", None, None),
        P(None, "row", None),
        P(None, None, "col"),
        P("row", "col"),
    )
    return jax.shard_map(
        body, mesh=mesh, in_specs=placed, out_specs=P("row", "col", None, None), check_vma=False
    )
```

```python
import functools

import jax
import jax.numpy as jnp
from jax import lax
from jax.experimental import pallas as pl
from jax.experimental.pallas import tpu as pltpu
from jax.sharding import PartitionSpec as P

CHUNKS = 4
MESH = pl.DeviceIdType.MESH


def matmul(a, b):
    return jnp.dot(a, b, preferred_element_type=jnp.float32)


def matmul_tn(a, b):
    return lax.dot_general(a, b, (((0,), (0,)), ((), ())), preferred_element_type=jnp.float32)


def matmul_nt(a, b):
    return lax.dot_general(a, b, (((1,), (1,)), ((), ())), preferred_element_type=jnp.float32)


def children(index, extent, minor, source):
    x, m = lax.rem(index, minor), lax.div(index, minor)
    found = [((x == source) & (m + 1 < extent // minor), index + minor)]
    if source + 1 < minor:
        found.append(((x >= source) & (x + 1 < minor), index + 1))
    if source > 0:
        found.append(((x <= source) & (x >= 1), index - 1))
    return found


def kernel(
    n_row, n_col, minor_col, ranks, left, right, lower, upper, out,
    ul, col_u, col_y, row_y, row_u, low, up,
    send_sem, recv_sem, inv_send, low_recv, up_recv, fetch_sem,
):
    r, c = lax.axis_index("row"), lax.axis_index("col")
    order, width = left.shape[2], left.shape[3]
    step = order // CHUNKS
    fetch_left = [
        [pltpu.make_async_copy(left.at[a, b], ul.at[a, b], fetch_sem.at[0, a, b]) for b in range(2)]
        for a in range(2)
    ]
    fetch_right = [
        [pltpu.make_async_copy(right.at[a, b], out.at[a, b], fetch_sem.at[1, a, b]) for b in range(2)]
        for a in range(2)
    ]
    every = [(a, b) for b in range(2) for a in range(2)]
    for a, b in every:
        fetch_left[a][b].start()
        fetch_right[a][b].start()

    barrier = pltpu.get_barrier_semaphore()
    for d in range(1, n_row):
        pl.semaphore_signal(
            barrier, inc=1, device_id={"row": lax.rem(r + d, n_row)}, device_id_type=MESH
        )
    for d in range(1, n_col):
        pl.semaphore_signal(
            barrier, inc=1, device_id={"col": lax.rem(c + d, n_col)}, device_id_type=MESH
        )

    own_rows = {"up": upper.shape[1], "low": lower.shape[1]}

    def own_up(k):
        rows = own_rows["up"]
        return pltpu.make_async_copy(upper.at[k], up.at[pl.ds(k * rows, rows)], inv_send.at[0, k])

    def own_low(k):
        rows = own_rows["low"]
        return pltpu.make_async_copy(lower.at[k], low.at[pl.ds(k * rows, rows)], inv_send.at[1, k])

    for k in range(2):

        @pl.when(c == k)
        def _():
            own_up(k).start()

        @pl.when(r == k)
        def _():
            own_low(k).start()

    lanes = lax.broadcasted_iota(jnp.int32, (1, width), 1)

    def keep(a, b):
        return (lanes < ranks[a, b]).astype(jnp.float32).astype(jnp.bfloat16)

    for a, b in every:
        mask = keep(a, b)
        fetch_left[a][b].wait()
        ul[a, b] = ul[a, b] * mask
        fetch_right[a][b].wait()
        out[a, b] = out[a, b] * mask
    for k in range(2):

        @pl.when(c == k)
        def _():
            for a in range(2):
                col_u[k, a] = ul[a, 0]

    @pl.when(r == 0)
    def _():
        for b in range(2):
            row_y[0, b] = out[0, b]

    pl.semaphore_wait(barrier, n_row - 1 + n_col - 1)

    buffers = {"cu": col_u, "cy": col_y, "ru": row_u, "ry": row_y}
    place = {
        (kind, k, t): n
        for n, (kind, k, t) in enumerate(
            (kind, k, t) for kind in ("cu", "cy", "ru", "ry") for k in range(2) for t in range(2)
        )
    }

    def axis_of(item):
        return "col" if item[0][0] == "c" else "row"

    def tree(item):
        if axis_of(item) == "col":
            return children(c, n_col, minor_col, item[1])
        return children(r, n_row, 2, item[1])

    def copy_of(item, chunk, way, target):
        kind, k, t = item
        view = buffers[kind].at[k, t, pl.ds(chunk * step, step)]
        return pltpu.make_async_remote_copy(
            src_ref=view,
            dst_ref=view,
            send_sem=send_sem.at[place[item], chunk, way],
            recv_sem=recv_sem.at[place[item], chunk],
            device_id={axis_of(item): target},
            device_id_type=MESH,
        )

    def wanted(item):
        kind, k, t = item
        if t > 0:
            return True
        return (r if axis_of(item) == "col" else c) > k

    def is_source(item):
        return (c if axis_of(item) == "col" else r) == item[1]

    def is_main(item):
        if axis_of(item) == "col":
            return lax.rem(c, minor_col) == item[1]
        return lax.rem(r, 2) == item[1]

    def forward(item, chunk):
        for way, (needed, target) in enumerate(tree(item)):

            @pl.when(needed)
            def _():
                copy_of(item, chunk, way, target).start()

    def send(item):
        @pl.when(is_source(item) & wanted(item))
        def _():
            for chunk in range(CHUNKS):
                forward(item, chunk)

    def relay(items, also=True):
        for chunk in range(CHUNKS):
            for item, main in items:
                role = is_main(item) if main else jnp.logical_not(is_main(item))

                @pl.when(jnp.logical_not(is_source(item)) & wanted(item) & role & also)
                def _():
                    copy_of(item, chunk, 0, 0).wait_recv()
                    forward(item, chunk)

    def main(*items):
        relay([(item, True) for item in items])

    def leaf(*items, also=True):
        relay([(item, False) for item in items], also)

    def up_copy(k, source):
        rows = upper.shape[1]
        return pltpu.make_async_remote_copy(
            src_ref=upper.at[k],
            dst_ref=up.at[pl.ds(pl.multiple_of(source * rows, rows), rows)],
            send_sem=inv_send.at[0, k],
            recv_sem=up_recv.at[source],
            device_id={"col": k},
            device_id_type=MESH,
        )

    def low_copy(k, source):
        rows = lower.shape[1]
        return pltpu.make_async_remote_copy(
            src_ref=lower.at[k],
            dst_ref=low.at[pl.ds(pl.multiple_of(source * rows, rows), rows)],
            send_sem=inv_send.at[1, k],
            recv_sem=low_recv.at[source],
            device_id={"row": k},
            device_id_type=MESH,
        )

    for k in range(2):

        @pl.when(c != k)
        def _():
            up_copy(k, c).start()

        @pl.when(r != k)
        def _():
            low_copy(k, r).start()

    send(("cu", 0, 0))
    send(("cu", 1, 0))
    for b in range(2):
        send(("ry", 0, b))

    for k in range(2):

        @pl.when(c == k)
        def _():
            own_up(k).wait()

        @pl.when(r == k)
        def _():
            own_low(k).wait()

    @pl.when(c < 2)
    def _():
        for s in range(n_col):

            @pl.when(s != c)
            def _():
                up_copy(0, s).wait_recv()

    @pl.when(c == 0)
    def _():
        col_y[0, 0] = matmul(up[...], out[0, 0]).astype(jnp.bfloat16)

    send(("cy", 0, 0))
    send(("cu", 0, 1))
    send(("cu", 1, 1))

    @pl.when(c == 0)
    def _():
        col_y[0, 1] = matmul(up[...], out[1, 0]).astype(jnp.bfloat16)

    send(("cy", 0, 1))

    @pl.when(r < 2)
    def _():
        for s in range(n_row):

            @pl.when(s != r)
            def _():
                low_copy(0, s).wait_recv()

    for b in range(2):
        for k in range(2):

            @pl.when(r == k)
            def _():
                row_u[k, b] = matmul(low[...], ul[0, b]).astype(jnp.bfloat16)

            send(("ru", k, b))

    def update(panel, a, b, also=True):
        row_in = (a * n_row + r) > panel
        tile_col = b * n_col + c

        @pl.when(row_in & (tile_col > panel) & also)
        def _():
            core = matmul_tn(col_y[panel, a], row_u[panel, b]).astype(jnp.bfloat16)
            meet = matmul_tn(ul[a, b], col_u[panel, a]).astype(jnp.bfloat16)
            mixed = matmul(meet, core).astype(jnp.bfloat16)
            change = matmul_nt(row_y[panel, b], mixed)
            out[a, b] = (out[a, b].astype(jnp.float32) - change).astype(jnp.bfloat16)

        if b == 0:

            @pl.when(row_in & (c == panel) & also)
            def _():
                out[a, 0] = col_y[panel, a]

    def solve_next(a):
        @pl.when(c == 1)
        def _():
            col_y[1, a] = matmul(up[...], out[a, 0]).astype(jnp.bfloat16)

        send(("cy", 1, a))

    def share_row(b):
        @pl.when(r == 1)
        def _():
            row_y[1, b] = out[0, b]

        send(("ry", 1, b))

    main(("cu", 0, 0), ("cu", 1, 0), ("ry", 0, 0), ("ru", 1, 0))
    main(("cy", 0, 0), ("cu", 1, 1), ("ru", 0, 0), ("ru", 1, 1))
    leaf(("cu", 0, 0), ("ry", 0, 0))
    leaf(("cy", 0, 0), ("ru", 0, 0))
    update(0, 0, 0)
    solve_next(0)
    share_row(0)
    leaf(("ry", 0, 1), ("ru", 0, 1), also=r == 1)
    update(0, 0, 1, also=r == 1)
    share_row(1)
    main(("cu", 0, 1), ("cy", 1, 0), ("ry", 0, 1), ("ry", 1, 0))
    main(("cy", 0, 1), ("ru", 0, 1), ("ry", 1, 1))
    leaf(("cu", 0, 1))
    leaf(("cy", 0, 1))
    update(0, 1, 0)
    solve_next(1)
    leaf(("ry", 0, 1), ("ru", 0, 1), also=r != 1)
    update(0, 0, 1, also=r != 1)
    update(0, 1, 1)
    main(("cy", 1, 1))
    leaf(("cu", 1, 0), ("cy", 1, 0), ("ru", 1, 0), ("ry", 1, 0))
    update(1, 0, 0)
    leaf(("ru", 1, 1), ("ry", 1, 1), ("cu", 1, 1))
    update(1, 0, 1)
    leaf(("cy", 1, 1))
    update(1, 1, 0)
    update(1, 1, 1)

    for k in range(2):

        @pl.when(c != k)
        def _():
            up_copy(k, c).wait_send()

        @pl.when(r != k)
        def _():
            low_copy(k, r).wait_send()

    for item in place:
        for way, (needed, target) in enumerate(tree(item)):

            @pl.when(needed & wanted(item))
            def _():
                for chunk in range(CHUNKS):
                    copy_of(item, chunk, way, target).wait_send()


def body(left, right, lower_inverse, upper_inverse, ranks):
    n_row, n_col = lax.axis_size("row"), lax.axis_size("col")
    minor_col = 4 if n_col % 4 == 0 and n_col > 8 else 2
    order, width = left.shape[2:]
    upper = jnp.swapaxes(upper_inverse, 1, 2)
    tile = (order, width)
    vmem = pl.BlockSpec(memory_space=pltpu.VMEM)
    hbm = pl.BlockSpec(memory_space=pltpu.HBM)
    return pl.pallas_call(
        functools.partial(kernel, n_row, n_col, minor_col),
        out_shape=jax.ShapeDtypeStruct(right.shape, jnp.bfloat16),
        in_specs=[pl.BlockSpec(memory_space=pltpu.SMEM)] + [hbm] * 4,
        out_specs=vmem,
        scratch_shapes=[
            pltpu.VMEM((2, 2) + tile, jnp.bfloat16),
            pltpu.VMEM((2, 2) + tile, jnp.bfloat16),
            pltpu.VMEM((2, 2) + tile, jnp.bfloat16),
            pltpu.VMEM((2, 2) + tile, jnp.bfloat16),
            pltpu.VMEM((2, 2) + tile, jnp.bfloat16),
            pltpu.VMEM((order, order), jnp.bfloat16),
            pltpu.VMEM((order, order), jnp.bfloat16),
            pltpu.SemaphoreType.DMA((16, CHUNKS, 3)),
            pltpu.SemaphoreType.DMA((16, CHUNKS)),
            pltpu.SemaphoreType.DMA((2, 2)),
            pltpu.SemaphoreType.DMA((n_row,)),
            pltpu.SemaphoreType.DMA((n_col,)),
            pltpu.SemaphoreType.DMA((2, 2, 2)),
        ],
        compiler_params=pltpu.CompilerParams(
            collective_id=0, has_side_effects=True, vmem_limit_bytes=40 * 1024 * 1024
        ),
        cost_estimate=pl.CostEstimate(
            flops=2_000_000_000, bytes_accessed=4_000_000, transcendentals=0
        ),
    )(ranks, left, right, lower_inverse, upper)


def solution(mesh):
    placed = (
        P("row", "col", None, None),
        P("row", "col", None, None),
        P(None, "row", None),
        P(None, None, "col"),
        P("row", "col"),
    )
    return jax.shard_map(
        body, mesh=mesh, in_specs=placed, out_specs=P("row", "col", None, None), check_vma=False
    )
```

```python
import functools

import jax
import jax.numpy as jnp
from jax import lax
from jax.experimental import pallas as pl
from jax.experimental.pallas import tpu as pltpu
from jax.sharding import PartitionSpec as P

CHUNKS = 4
MESH = pl.DeviceIdType.MESH


def matmul(a, b):
    return jnp.dot(a, b, preferred_element_type=jnp.float32)


def matmul_tn(a, b):
    return lax.dot_general(a, b, (((0,), (0,)), ((), ())), preferred_element_type=jnp.float32)


def matmul_nt(a, b):
    return lax.dot_general(a, b, (((1,), (1,)), ((), ())), preferred_element_type=jnp.float32)


def children(index, extent, minor, source):
    x, m = lax.rem(index, minor), lax.div(index, minor)
    found = [((x == source) & (m + 1 < extent // minor), index + minor)]
    if source + 1 < minor:
        found.append(((x >= source) & (x + 1 < minor), index + 1))
    if source > 0:
        found.append(((x <= source) & (x >= 1), index - 1))
    return found


def kernel(
    n_row, n_col, minor_col, ranks, left, right, lower, upper, out,
    ul, col_u, col_y, row_y, row_u, low, up,
    send_sem, recv_sem, inv_send, low_recv, up_recv, fetch_sem, swap_sem,
):
    r, c = lax.axis_index("row"), lax.axis_index("col")
    order, width = left.shape[2], left.shape[3]
    step = order // CHUNKS
    fetch_left = [
        [pltpu.make_async_copy(left.at[a, b], ul.at[a, b], fetch_sem.at[0, a, b]) for b in range(2)]
        for a in range(2)
    ]
    fetch_right = [
        [pltpu.make_async_copy(right.at[a, b], out.at[a, b], fetch_sem.at[1, a, b]) for b in range(2)]
        for a in range(2)
    ]
    every = [(1, 0), (0, 0), (0, 1), (1, 1)]
    for a, b in every:
        fetch_left[a][b].start()
    for a, b in every:
        fetch_right[a][b].start()

    barrier = pltpu.get_barrier_semaphore()
    for d in range(1, n_row):
        pl.semaphore_signal(
            barrier, inc=1, device_id={"row": lax.rem(r + d, n_row)}, device_id_type=MESH
        )
    for d in range(1, n_col):
        pl.semaphore_signal(
            barrier, inc=1, device_id={"col": lax.rem(c + d, n_col)}, device_id_type=MESH
        )

    own_rows = {"up": upper.shape[1], "low": lower.shape[1]}

    def own_up(k):
        rows = own_rows["up"]
        half = pl.ds(pl.multiple_of(lax.rem(r, 2) * (order // 2), order // 2), order // 2)
        return pltpu.make_async_copy(
            upper.at[k, :, half], up.at[pl.ds(k * rows, rows), half], inv_send.at[0, k]
        )

    def own_low(k):
        rows = own_rows["low"]
        return pltpu.make_async_copy(lower.at[k], low.at[pl.ds(k * rows, rows)], inv_send.at[1, k])

    for k in range(2):

        @pl.when(c == k)
        def _():
            own_up(k).start()

        @pl.when(r == k)
        def _():
            own_low(k).start()

    lanes = lax.broadcasted_iota(jnp.int32, (1, width), 1)

    def keep(a, b):
        return (lanes < ranks[a, b]).astype(jnp.float32).astype(jnp.bfloat16)

    buffers = {"cu": col_u, "cy": col_y, "ru": row_u, "ry": row_y}
    place = {
        (kind, k, t): n
        for n, (kind, k, t) in enumerate(
            (kind, k, t) for kind in ("cu", "cy", "ru", "ry") for k in range(2) for t in range(2)
        )
    }

    def axis_of(item):
        return "col" if item[0][0] == "c" else "row"

    def tree(item):
        if axis_of(item) == "col":
            return children(c, n_col, minor_col, item[1])
        return children(r, n_row, 2, item[1])

    def copy_of(item, chunk, way, target):
        kind, k, t = item
        view = buffers[kind].at[k, t, pl.ds(chunk * step, step)]
        return pltpu.make_async_remote_copy(
            src_ref=view,
            dst_ref=view,
            send_sem=send_sem.at[place[item], chunk, way],
            recv_sem=recv_sem.at[place[item], chunk],
            device_id={axis_of(item): target},
            device_id_type=MESH,
        )

    def wanted(item):
        kind, k, t = item
        if t > 0:
            return True
        return (r if axis_of(item) == "col" else c) > k

    def is_source(item):
        return (c if axis_of(item) == "col" else r) == item[1]

    def is_main(item):
        if axis_of(item) == "col":
            return lax.rem(c, minor_col) == item[1]
        return lax.rem(r, 2) == item[1]

    def forward(item, chunk):
        for way, (needed, target) in enumerate(tree(item)):

            @pl.when(needed)
            def _():
                copy_of(item, chunk, way, target).start()

    def send(item, also=True):
        @pl.when(is_source(item) & wanted(item) & also)
        def _():
            for chunk in range(CHUNKS):
                forward(item, chunk)

    def relay(items, also=True):
        for chunk in range(CHUNKS):
            for item, main in items:
                role = is_main(item) if main else jnp.logical_not(is_main(item))

                @pl.when(jnp.logical_not(is_source(item)) & wanted(item) & role & also)
                def _():
                    copy_of(item, chunk, 0, 0).wait_recv()
                    forward(item, chunk)

    def main(*items, also=True):
        relay([(item, True) for item in items], also)

    def leaf(*items, also=True):
        relay([(item, False) for item in items], also)

    half = order // 2
    mine = pl.ds(pl.multiple_of(lax.rem(r, 2) * half, half), half)

    def swap_halves():
        return pltpu.make_async_remote_copy(
            src_ref=up.at[:, mine],
            dst_ref=up.at[:, mine],
            send_sem=swap_sem.at[0],
            recv_sem=swap_sem.at[1],
            device_id={"row": r + 1 - 2 * lax.rem(r, 2)},
            device_id_type=MESH,
        )

    def up_copy(k, source):
        rows = upper.shape[1]
        return pltpu.make_async_remote_copy(
            src_ref=upper.at[k, :, mine],
            dst_ref=up.at[pl.ds(pl.multiple_of(source * rows, rows), rows), mine],
            send_sem=inv_send.at[0, k],
            recv_sem=up_recv.at[source],
            device_id={"col": k},
            device_id_type=MESH,
        )

    def low_copy(k, source):
        rows = lower.shape[1]
        return pltpu.make_async_remote_copy(
            src_ref=lower.at[k],
            dst_ref=low.at[pl.ds(pl.multiple_of(source * rows, rows), rows)],
            send_sem=inv_send.at[1, k],
            recv_sem=low_recv.at[source],
            device_id={"row": k},
            device_id_type=MESH,
        )

    for a in range(2):
        fetch_left[a][0].wait()
        ul[a, 0] = ul[a, 0] * keep(a, 0)
        for k in range(2):

            @pl.when(c == k)
            def _():
                col_u[k, a] = ul[a, 0]

    pl.semaphore_wait(barrier, n_row - 1 + n_col - 1)

    for k in range(2):

        @pl.when(c != k)
        def _():
            up_copy(k, c).start()

        @pl.when(r != k)
        def _():
            low_copy(k, r).start()

    send(("cu", 0, 0))
    send(("cu", 0, 1), also=r >= 2)
    send(("cu", 1, 0))
    send(("cu", 1, 1))
    for a, b in ((0, 0), (0, 1), (1, 0), (1, 1)):
        fetch_right[a][b].wait()
        out[a, b] = out[a, b] * keep(a, b)
        if a == 0:

            @pl.when(r == 0)
            def _():
                row_y[0, b] = out[0, b]

            send(("ry", 0, b))
    for a, b in ((0, 1), (1, 1)):
        fetch_left[a][b].wait()
        ul[a, b] = ul[a, b] * keep(a, b)

    for k in range(2):

        @pl.when(c == k)
        def _():
            own_up(k).wait()

        @pl.when(r == k)
        def _():
            own_low(k).wait()

    @pl.when(c < 2)
    def _():
        for s in range(n_col):

            @pl.when(s != c)
            def _():
                up_copy(0, s).wait_recv()

        swap_halves().start()
        swap_halves().wait_recv()

    @pl.when(c == 0)
    def _():
        col_y[0, 0] = matmul(up[...], out[0, 0]).astype(jnp.bfloat16)

    send(("cy", 0, 0))
    send(("cu", 0, 1), also=r < 2)

    @pl.when(c == 0)
    def _():
        col_y[0, 1] = matmul(up[...], out[1, 0]).astype(jnp.bfloat16)

    send(("cy", 0, 1))

    @pl.when(r < 2)
    def _():
        for s in range(n_row):

            @pl.when(s != r)
            def _():
                low_copy(0, s).wait_recv()

    for b in range(2):
        for k in range(2):

            @pl.when(r == k)
            def _():
                row_u[k, b] = matmul(low[...], ul[0, b]).astype(jnp.bfloat16)

            send(("ru", k, b))

    def update(panel, a, b, also=True):
        row_in = (a * n_row + r) > panel
        tile_col = b * n_col + c

        @pl.when(row_in & (tile_col > panel) & also)
        def _():
            core = matmul_tn(col_y[panel, a], row_u[panel, b]).astype(jnp.bfloat16)
            meet = matmul_tn(ul[a, b], col_u[panel, a]).astype(jnp.bfloat16)
            mixed = matmul(meet, core).astype(jnp.bfloat16)
            change = matmul_nt(row_y[panel, b], mixed)
            out[a, b] = (out[a, b].astype(jnp.float32) - change).astype(jnp.bfloat16)

        if b == 0:

            @pl.when(row_in & (c == panel) & also)
            def _():
                out[a, 0] = col_y[panel, a]

    def solve_next(a):
        @pl.when(c == 1)
        def _():
            col_y[1, a] = matmul(up[...], out[a, 0]).astype(jnp.bfloat16)

        send(("cy", 1, a))

    def share_row(b):
        @pl.when(r == 1)
        def _():
            row_y[1, b] = out[0, b]

        send(("ry", 1, b))

    main(("cu", 0, 0), ("cu", 1, 0), ("ry", 0, 0))
    main(("cy", 0, 0), also=r < 2)
    leaf(("cu", 0, 0), ("ry", 0, 0), ("cy", 0, 0), ("ru", 0, 0), also=r == 1)
    update(0, 0, 0, also=r == 1)
    share_row(0)
    leaf(("ry", 0, 1), ("ru", 0, 1), also=r == 1)
    update(0, 0, 1, also=r == 1)
    share_row(1)
    main(("cu", 0, 1), ("cu", 1, 1), ("ry", 0, 1))
    main(("cy", 0, 0), ("ru", 0, 0), also=r >= 2)
    main(("ru", 1, 0))
    leaf(("cu", 0, 0), ("ry", 0, 0), ("cy", 0, 0), ("ru", 0, 0), also=r != 1)
    update(0, 0, 0, also=r != 1)
    solve_next(0)
    main(("cy", 0, 1), ("cy", 1, 0), ("ru", 0, 1), ("ru", 1, 1))
    leaf(("cu", 0, 1))
    leaf(("cy", 0, 1))
    update(0, 1, 0)
    solve_next(1)
    leaf(("ry", 0, 1), ("ru", 0, 1), also=r != 1)
    update(0, 0, 1, also=r != 1)
    update(0, 1, 1)
    main(("cy", 1, 1), ("ry", 1, 0))
    main(("ry", 1, 1))
    leaf(("cu", 1, 0), ("cy", 1, 0), ("ru", 1, 0), ("ry", 1, 0))
    update(1, 0, 0)
    leaf(("ru", 1, 1), ("ry", 1, 1), ("cu", 1, 1))
    update(1, 0, 1)
    leaf(("cy", 1, 1))
    update(1, 1, 0)
    update(1, 1, 1)

    for k in range(2):

        @pl.when(c != k)
        def _():
            up_copy(k, c).wait_send()

        @pl.when(r != k)
        def _():
            low_copy(k, r).wait_send()

    @pl.when(c < 2)
    def _():
        swap_halves().wait_send()

    for item in place:
        for way, (needed, target) in enumerate(tree(item)):

            @pl.when(needed & wanted(item))
            def _():
                for chunk in range(CHUNKS):
                    copy_of(item, chunk, way, target).wait_send()


def body(left, right, lower_inverse, upper_inverse, ranks):
    n_row, n_col = lax.axis_size("row"), lax.axis_size("col")
    minor_col = 4 if n_col % 4 == 0 and n_col > 8 else 2
    order, width = left.shape[2:]
    upper = jnp.swapaxes(upper_inverse, 1, 2)
    tile = (order, width)
    vmem = pl.BlockSpec(memory_space=pltpu.VMEM)
    hbm = pl.BlockSpec(memory_space=pltpu.HBM)
    return pl.pallas_call(
        functools.partial(kernel, n_row, n_col, minor_col),
        out_shape=jax.ShapeDtypeStruct(right.shape, jnp.bfloat16),
        in_specs=[pl.BlockSpec(memory_space=pltpu.SMEM)] + [hbm] * 4,
        out_specs=vmem,
        scratch_shapes=[
            pltpu.VMEM((2, 2) + tile, jnp.bfloat16),
            pltpu.VMEM((2, 2) + tile, jnp.bfloat16),
            pltpu.VMEM((2, 2) + tile, jnp.bfloat16),
            pltpu.VMEM((2, 2) + tile, jnp.bfloat16),
            pltpu.VMEM((2, 2) + tile, jnp.bfloat16),
            pltpu.VMEM((order, order), jnp.bfloat16),
            pltpu.VMEM((order, order), jnp.bfloat16),
            pltpu.SemaphoreType.DMA((16, CHUNKS, 3)),
            pltpu.SemaphoreType.DMA((16, CHUNKS)),
            pltpu.SemaphoreType.DMA((2, 2)),
            pltpu.SemaphoreType.DMA((n_row,)),
            pltpu.SemaphoreType.DMA((n_col,)),
            pltpu.SemaphoreType.DMA((2, 2, 2)),
            pltpu.SemaphoreType.DMA((2,)),
        ],
        compiler_params=pltpu.CompilerParams(
            collective_id=0, has_side_effects=True, vmem_limit_bytes=60 * 1024 * 1024
        ),
        cost_estimate=pl.CostEstimate(
            flops=2_000_000_000, bytes_accessed=4_000_000, transcendentals=0
        ),
    )(ranks, left, right, lower_inverse, upper)


def solution(mesh):
    placed = (
        P("row", "col", None, None),
        P("row", "col", None, None),
        P(None, "row", None),
        P(None, None, "col"),
        P("row", "col"),
    )
    return jax.shard_map(
        body, mesh=mesh, in_specs=placed, out_specs=P("row", "col", None, None), check_vma=False
    )
```

```python
import functools

import jax
import jax.numpy as jnp
from jax import lax
from jax.experimental import pallas as pl
from jax.experimental.pallas import tpu as pltpu
from jax.sharding import PartitionSpec as P

CHUNKS = 4
MESH = pl.DeviceIdType.MESH


def matmul(a, b):
    return jnp.dot(a, b, preferred_element_type=jnp.float32)


def matmul_tn(a, b):
    return lax.dot_general(a, b, (((0,), (0,)), ((), ())), preferred_element_type=jnp.float32)


def matmul_nt(a, b):
    return lax.dot_general(a, b, (((1,), (1,)), ((), ())), preferred_element_type=jnp.float32)


def children(index, extent, minor, source):
    x, m = lax.rem(index, minor), lax.div(index, minor)
    found = [((x == source) & (m + 1 < extent // minor), index + minor)]
    if source + 1 < minor:
        found.append(((x >= source) & (x + 1 < minor), index + 1))
    if source > 0:
        found.append(((x <= source) & (x >= 1), index - 1))
    return found


def kernel(
    n_row, n_col, minor_col, ranks, left, right, lower, upper, out,
    ul, col_u, col_y, row_y, row_u, low, up,
    send_sem, recv_sem, inv_send, low_recv, up_recv, fetch_sem, swap_sem,
):
    r, c = lax.axis_index("row"), lax.axis_index("col")
    order, width = left.shape[2], left.shape[3]
    step = order // CHUNKS
    fetch_left = [
        [pltpu.make_async_copy(left.at[a, b], ul.at[a, b], fetch_sem.at[0, a, b]) for b in range(2)]
        for a in range(2)
    ]
    fetch_right = [
        [pltpu.make_async_copy(right.at[a, b], out.at[a, b], fetch_sem.at[1, a, b]) for b in range(2)]
        for a in range(2)
    ]
    every = [(1, 0), (0, 0), (0, 1), (1, 1)]
    for a, b in every:
        fetch_left[a][b].start()
    for a, b in every:
        fetch_right[a][b].start()

    barrier = pltpu.get_barrier_semaphore()
    for d in range(1, n_row):
        pl.semaphore_signal(
            barrier, inc=1, device_id={"row": lax.rem(r + d, n_row)}, device_id_type=MESH
        )
    for d in range(1, n_col):
        pl.semaphore_signal(
            barrier, inc=1, device_id={"col": lax.rem(c + d, n_col)}, device_id_type=MESH
        )

    own_rows = {"up": upper.shape[1], "low": lower.shape[1]}

    def own_up(k):
        rows = own_rows["up"]
        half = pl.ds(pl.multiple_of(lax.rem(r, 2) * (order // 2), order // 2), order // 2)
        return pltpu.make_async_copy(
            upper.at[k, :, half], up.at[pl.ds(k * rows, rows), half], inv_send.at[0, k]
        )

    def own_low(k):
        rows = own_rows["low"]
        return pltpu.make_async_copy(lower.at[k], low.at[pl.ds(k * rows, rows)], inv_send.at[1, k])

    for k in range(2):

        @pl.when(c == k)
        def _():
            own_up(k).start()

        @pl.when(r == k)
        def _():
            own_low(k).start()

    lanes = lax.broadcasted_iota(jnp.int32, (1, width), 1)

    def keep(a, b):
        return (lanes < ranks[a, b]).astype(jnp.float32).astype(jnp.bfloat16)

    buffers = {"cu": col_u, "cy": col_y, "ru": row_u, "ry": row_y}
    place = {
        (kind, k, t): n
        for n, (kind, k, t) in enumerate(
            (kind, k, t) for kind in ("cu", "cy", "ru", "ry") for k in range(2) for t in range(2)
        )
    }

    def axis_of(item):
        return "col" if item[0][0] == "c" else "row"

    def tree(item):
        if axis_of(item) == "col":
            return children(c, n_col, minor_col, item[1])
        return children(r, n_row, 2, item[1])

    def copy_of(item, chunk, way, target):
        kind, k, t = item
        view = buffers[kind].at[k, t, pl.ds(chunk * step, step)]
        return pltpu.make_async_remote_copy(
            src_ref=view,
            dst_ref=view,
            send_sem=send_sem.at[place[item], chunk, way],
            recv_sem=recv_sem.at[place[item], chunk],
            device_id={axis_of(item): target},
            device_id_type=MESH,
        )

    def wanted(item):
        kind, k, t = item
        if t > 0:
            return True
        return (r if axis_of(item) == "col" else c) > k

    def is_source(item):
        return (c if axis_of(item) == "col" else r) == item[1]

    def is_main(item):
        if axis_of(item) == "col":
            return lax.rem(c, minor_col) == item[1]
        return lax.rem(r, 2) == item[1]

    def forward(item, chunk):
        for way, (needed, target) in enumerate(tree(item)):

            @pl.when(needed)
            def _():
                copy_of(item, chunk, way, target).start()

    def send(item, also=True):
        @pl.when(is_source(item) & wanted(item) & also)
        def _():
            for chunk in range(CHUNKS):
                forward(item, chunk)

    def relay(items, also=True, chunks=range(CHUNKS)):
        for chunk in chunks:
            for item, main in items:
                role = is_main(item) if main else jnp.logical_not(is_main(item))

                @pl.when(jnp.logical_not(is_source(item)) & wanted(item) & role & also)
                def _():
                    copy_of(item, chunk, 0, 0).wait_recv()
                    forward(item, chunk)

    def main(*items, also=True):
        relay([(item, True) for item in items], also)

    def leaf(*items, also=True):
        relay([(item, False) for item in items], also)

    half = order // 2
    mine = pl.ds(pl.multiple_of(lax.rem(r, 2) * half, half), half)

    def swap_halves():
        return pltpu.make_async_remote_copy(
            src_ref=up.at[:, mine],
            dst_ref=up.at[:, mine],
            send_sem=swap_sem.at[0],
            recv_sem=swap_sem.at[1],
            device_id={"row": r + 1 - 2 * lax.rem(r, 2)},
            device_id_type=MESH,
        )

    def up_copy(k, source):
        rows = upper.shape[1]
        return pltpu.make_async_remote_copy(
            src_ref=upper.at[k, :, mine],
            dst_ref=up.at[pl.ds(pl.multiple_of(source * rows, rows), rows), mine],
            send_sem=inv_send.at[0, k],
            recv_sem=up_recv.at[source],
            device_id={"col": k},
            device_id_type=MESH,
        )

    def low_copy(k, source):
        rows = lower.shape[1]
        return pltpu.make_async_remote_copy(
            src_ref=lower.at[k],
            dst_ref=low.at[pl.ds(pl.multiple_of(source * rows, rows), rows)],
            send_sem=inv_send.at[1, k],
            recv_sem=low_recv.at[source],
            device_id={"row": k},
            device_id_type=MESH,
        )

    for a in range(2):
        fetch_left[a][0].wait()
        ul[a, 0] = ul[a, 0] * keep(a, 0)
        for k in range(2):

            @pl.when(c == k)
            def _():
                col_u[k, a] = ul[a, 0]

    pl.semaphore_wait(barrier, n_row - 1 + n_col - 1)

    for k in range(2):

        @pl.when(c != k)
        def _():
            up_copy(k, c).start()

        @pl.when(r != k)
        def _():
            low_copy(k, r).start()

    send(("cu", 0, 0))
    send(("cu", 0, 1), also=r >= 2)
    send(("cu", 1, 0))
    send(("cu", 1, 1))
    for a, b in ((0, 0), (0, 1), (1, 0), (1, 1)):
        fetch_right[a][b].wait()
        out[a, b] = out[a, b] * keep(a, b)
        if a == 0:

            @pl.when(r == 0)
            def _():
                row_y[0, b] = out[0, b]

            send(("ry", 0, b))
    for a, b in ((0, 1), (1, 1)):
        fetch_left[a][b].wait()
        ul[a, b] = ul[a, b] * keep(a, b)

    for k in range(2):

        @pl.when(c == k)
        def _():
            own_up(k).wait()

        @pl.when(r == k)
        def _():
            own_low(k).wait()

    @pl.when(c < 2)
    def _():
        for s in range(n_col):

            @pl.when(s != c)
            def _():
                up_copy(0, s).wait_recv()

        swap_halves().start()
        swap_halves().wait_recv()

    @pl.when(c == 0)
    def _():
        col_y[0, 0] = matmul(up[...], out[0, 0]).astype(jnp.bfloat16)

    send(("cy", 0, 0))
    send(("cu", 0, 1), also=r < 2)

    @pl.when(c == 0)
    def _():
        col_y[0, 1] = matmul(up[...], out[1, 0]).astype(jnp.bfloat16)

    send(("cy", 0, 1))

    @pl.when(r < 2)
    def _():
        for s in range(n_row):

            @pl.when(s != r)
            def _():
                low_copy(0, s).wait_recv()

    for b in range(2):
        for k in range(2):

            @pl.when(r == k)
            def _():
                row_u[k, b] = matmul(low[...], ul[0, b]).astype(jnp.bfloat16)

            send(("ru", k, b))

    def update(panel, a, b, also=True):
        row_in = (a * n_row + r) > panel
        tile_col = b * n_col + c

        @pl.when(row_in & (tile_col > panel) & also)
        def _():
            core = matmul_tn(col_y[panel, a], row_u[panel, b]).astype(jnp.bfloat16)
            meet = matmul_tn(ul[a, b], col_u[panel, a]).astype(jnp.bfloat16)
            mixed = matmul(meet, core).astype(jnp.bfloat16)
            change = matmul_nt(row_y[panel, b], mixed)
            out[a, b] = (out[a, b].astype(jnp.float32) - change).astype(jnp.bfloat16)

        if b == 0:

            @pl.when(row_in & (c == panel) & also)
            def _():
                out[a, 0] = col_y[panel, a]

    def solve_next(a):
        @pl.when(c == 1)
        def _():
            col_y[1, a] = matmul(up[...], out[a, 0]).astype(jnp.bfloat16)

        send(("cy", 1, a))

    def share_row(b):
        @pl.when(r == 1)
        def _():
            row_y[1, b] = out[0, b]

        send(("ry", 1, b))

    main(("cu", 0, 0), ("cu", 1, 0), ("ry", 0, 0))
    main(("cy", 0, 0), also=r < 2)
    leaf(("cu", 0, 0), ("ry", 0, 0), ("cy", 0, 0), ("ru", 0, 0), also=r == 1)
    update(0, 0, 0, also=r == 1)
    share_row(0)
    leaf(("ry", 0, 1), ("ru", 0, 1), also=r == 1)
    update(0, 0, 1, also=r == 1)
    share_row(1)
    main(("cu", 0, 1), ("cu", 1, 1), ("ry", 0, 1))
    main(("cy", 0, 0), ("ru", 0, 0), also=r >= 2)
    main(("ru", 1, 0))
    leaf(("cu", 0, 0), ("ry", 0, 0), ("cy", 0, 0), ("ru", 0, 0), also=r != 1)
    update(0, 0, 0, also=r != 1)
    solve_next(0)
    main(("cy", 0, 1), ("cy", 1, 0), ("ru", 0, 1), ("ru", 1, 1))
    leaf(("cu", 0, 1))
    leaf(("cy", 0, 1))
    update(0, 1, 0, also=c == 1)
    solve_next(1)
    leaf(("ry", 0, 1), ("ru", 0, 1), also=r != 1)
    quarter = CHUNKS // 4
    last = [range(quarter * n, quarter * (n + 1)) for n in range(4)]
    relay([(("cy", 1, 1), True)], chunks=last[0])
    update(0, 1, 0, also=c != 1)
    relay([(("cy", 1, 1), True)], chunks=last[1])
    update(0, 0, 1, also=r != 1)
    relay([(("cy", 1, 1), True)], chunks=last[2])
    update(0, 1, 1)
    relay([(("cy", 1, 1), True)], chunks=last[3])
    main(("ry", 1, 0))
    main(("ry", 1, 1))
    leaf(("cu", 1, 0), ("cy", 1, 0), ("ru", 1, 0), ("ry", 1, 0))
    update(1, 0, 0)
    leaf(("ru", 1, 1), ("ry", 1, 1), ("cu", 1, 1))
    update(1, 0, 1)
    leaf(("cy", 1, 1))
    update(1, 1, 0)
    update(1, 1, 1)

    for k in range(2):

        @pl.when(c != k)
        def _():
            up_copy(k, c).wait_send()

        @pl.when(r != k)
        def _():
            low_copy(k, r).wait_send()

    @pl.when(c < 2)
    def _():
        swap_halves().wait_send()

    for item in place:
        for way, (needed, target) in enumerate(tree(item)):

            @pl.when(needed & wanted(item))
            def _():
                for chunk in range(CHUNKS):
                    copy_of(item, chunk, way, target).wait_send()


def body(left, right, lower_inverse, upper_inverse, ranks):
    n_row, n_col = lax.axis_size("row"), lax.axis_size("col")
    minor_col = 4 if n_col % 4 == 0 and n_col > 8 else 2
    order, width = left.shape[2:]
    upper = jnp.swapaxes(upper_inverse, 1, 2)
    tile = (order, width)
    vmem = pl.BlockSpec(memory_space=pltpu.VMEM)
    hbm = pl.BlockSpec(memory_space=pltpu.HBM)
    return pl.pallas_call(
        functools.partial(kernel, n_row, n_col, minor_col),
        out_shape=jax.ShapeDtypeStruct(right.shape, jnp.bfloat16),
        in_specs=[pl.BlockSpec(memory_space=pltpu.SMEM)] + [hbm] * 4,
        out_specs=vmem,
        scratch_shapes=[
            pltpu.VMEM((2, 2) + tile, jnp.bfloat16),
            pltpu.VMEM((2, 2) + tile, jnp.bfloat16),
            pltpu.VMEM((2, 2) + tile, jnp.bfloat16),
            pltpu.VMEM((2, 2) + tile, jnp.bfloat16),
            pltpu.VMEM((2, 2) + tile, jnp.bfloat16),
            pltpu.VMEM((order, order), jnp.bfloat16),
            pltpu.VMEM((order, order), jnp.bfloat16),
            pltpu.SemaphoreType.DMA((16, CHUNKS, 3)),
            pltpu.SemaphoreType.DMA((16, CHUNKS)),
            pltpu.SemaphoreType.DMA((2, 2)),
            pltpu.SemaphoreType.DMA((n_row,)),
            pltpu.SemaphoreType.DMA((n_col,)),
            pltpu.SemaphoreType.DMA((2, 2, 2)),
            pltpu.SemaphoreType.DMA((2,)),
        ],
        compiler_params=pltpu.CompilerParams(
            collective_id=0, has_side_effects=True, vmem_limit_bytes=60 * 1024 * 1024
        ),
        cost_estimate=pl.CostEstimate(
            flops=2_000_000_000, bytes_accessed=4_000_000, transcendentals=0
        ),
    )(ranks, left, right, lower_inverse, upper)


def solution(mesh):
    placed = (
        P("row", "col", None, None),
        P("row", "col", None, None),
        P(None, "row", None),
        P(None, None, "col"),
        P("row", "col"),
    )
    return jax.shard_map(
        body, mesh=mesh, in_specs=placed, out_specs=P("row", "col", None, None), check_vma=False
    )
```
